32 devices in a mesh: groups: 2 (over y), ctx: 4 (over z), tp: 4 (over x, core).
Axes of the slice: x: 2, y: 2, z: 4, core: 2. Of those that a mesh axis runs over, the one named last changes fastest.
Arguments:
- queries: bfloat16 [64, 5120], P(('groups', 'ctx'), 'tp'), parts along dimension 0, may hold values from -12 to 12
- pool: bfloat16 [160, 2, 128, 1024], P(('groups', 'ctx'), None, None, 'tp'), parts along dimension 0, may hold values from -80 to 80
- resident: bfloat16 [4, 2, 512, 1024], P('groups', None, 'ctx', 'tp'), parts along dimension 0, may hold values from -6 to 6
- lengths: int32 [64], P(('groups', 'ctx')), parts along dimension 0, may hold values from 129 to 256
- table: int32 [64, 2], P(('groups', 'ctx')), parts along dimension 0, may hold values from 0 to 19, as said below
- moving_row_numbers: int32 [4], P('groups'), parts along dimension 0, may hold values from 0 to 31, as said below
- mover_table: int32 [4, 8], P('groups', 'ctx'), parts along dimension 0, may hold values from 0 to 19, as said below
- targets: int32 [4, 8], P('groups', 'ctx'), parts along dimension 0, may hold values from 0 to 3, as said below
Outputs:
- attended: bfloat16 [64, 5120], P(('groups', 'ctx'), 'tp'), parts along dimension 0
- received: bfloat16 [48, 2, 128, 1024], P(('groups', 'ctx'), None, None, 'tp'), parts along dimension 0
The draws below stay inside these ranges and needn't reach their ends.
There are 2 independent parts, one for each index of `groups`. The reference program is written for one: setup_inputs(seed, part) draws one part's arguments, and reference() takes and returns one part's arrays. A program takes and returns all parts, laid end to end along the dimension named above; each array names one. Nothing has to cross between parts.
Inputs may be any that keep to these rules, and one draw needn't show every extreme that they name: On each ctx shard, the 8 x 2 entries of table for its rows and the 2 x 2 entries of mover_table in its columns name each of its 20 pages once. `mover_table`: see table. `moving_row_numbers`: distinct rows; the last row, 31, is always among them. `targets`: A page of shard c goes to one of the shards c, c + 1, ..., c + 2, counted mod 4. Every shard sends exactly 2 of its moving pages to one shard and at most 2 to any shard; some shard takes 2 pages from each of the 3 shards that may send to it.
All inputs are finite; a program needn't handle non-finite values.
Results may differ from the reference program's by a relative error of at most 0.0031.
Values may be sent and summed in bfloat16 or wider, within the bound.
A program may use at most 64 MiB of HBM per device.

```python
import math
from functools import reduce
import jax
import jax.numpy as jnp
from jax import lax

QUERY_HEADS = 40
KEY_VALUE_HEADS = 8
HEAD_SIZE = 128
PAGE_TOKENS = 128
RBLK = 2
MBLK = 2
MOVING_SEQUENCES = 2
REACH = 3
SHARD_ROWS = 8
RESIDENT_COUNT = 128
DECODE_ROWS = 32
POOL_PAGES = 20
CAP = 2
ARRIVAL_SLOTS = 6
N_CTX = 4


def page_order(key):
    page_keys = jax.random.split(jax.random.fold_in(key, 5), N_CTX)

    def shuffle_one(one_key):
        return jax.random.permutation(one_key, POOL_PAGES)
    return jax.vmap(shuffle_one)(page_keys).astype(jnp.int32)


def base_queries(key):
    field_name = jax.random.truncated_normal(jax.random.fold_in(key, 7), -6.0, 6.0, (DECODE_ROWS, QUERY_HEADS * HEAD_SIZE), jnp.float32)
    return 2.0 * field_name


def draw_queries(key, part):
    shared_state = base_queries(key)
    return shared_state.astype(jnp.bfloat16)


def draw_table(key, part):
    orders = page_order(key)
    return orders[:, :SHARD_ROWS * RBLK].reshape(DECODE_ROWS, RBLK)


def draw_mover_table(key, part):
    orders = page_order(key)
    moving = orders[:, SHARD_ROWS * RBLK:].reshape(N_CTX, MOVING_SEQUENCES, MBLK)
    return moving.transpose(1, 0, 2).reshape(MOVING_SEQUENCES, N_CTX * MBLK)


def draw_moving_row_numbers(key, part):
    key = jax.random.fold_in(key, 2)
    key_rest, key_mix = jax.random.split(key, 2)
    rest = jax.random.permutation(key_rest, DECODE_ROWS - 1)[:MOVING_SEQUENCES - 1].astype(jnp.int32)
    rows = jnp.concatenate([jnp.full((1,), DECODE_ROWS - 1, jnp.int32), rest])
    return jax.random.permutation(key_mix, rows).astype(jnp.int32)


def draw_targets(key, part):
    key = jax.random.fold_in(key, 3)
    key_heavy, key_focus, key_other, key_mix = jax.random.split(key, 4)
    count = MOVING_SEQUENCES * MBLK
    shard_ids = jnp.arange(N_CTX, dtype=jnp.int32)
    heavy = jax.random.randint(key_heavy, (N_CTX,), 0, REACH)
    focus = jax.random.randint(key_focus, (), 0, N_CTX)
    behind = jnp.mod(focus - shard_ids, N_CTX)
    heavy = jnp.where(behind < REACH, behind, heavy)
    others = jnp.mod(heavy[:, None] + 1 + jax.random.randint(key_other, (N_CTX, count - CAP), 0, REACH - 1), REACH)
    offsets = jnp.concatenate([jnp.broadcast_to(heavy[:, None], (N_CTX, CAP)), others], axis=1)
    mix_keys = jax.random.split(key_mix, N_CTX)
    shuffled = jax.vmap(jax.random.permutation)(mix_keys, offsets)
    chosen = jnp.mod(shard_ids[:, None] + shuffled, N_CTX).reshape(N_CTX, MOVING_SEQUENCES, MBLK)
    return chosen.transpose(1, 0, 2).reshape(MOVING_SEQUENCES, N_CTX * MBLK).astype(jnp.int32)


def draw_pool(key, part):
    key = jax.random.fold_in(key, 4)
    array_shape = (N_CTX * POOL_PAGES, 2, PAGE_TOKENS, KEY_VALUE_HEADS, HEAD_SIZE)
    field_name = jax.random.truncated_normal(key, -6.0, 6.0, array_shape, jnp.float32)
    return field_name.reshape(N_CTX * POOL_PAGES, 2, PAGE_TOKENS, KEY_VALUE_HEADS * HEAD_SIZE).astype(jnp.bfloat16)


def plant(entries, own_key, low, top_value):
    extent = entries.shape
    spot = [jax.random.randint(jax.random.fold_in(own_key, axis), (), 0, extent[axis]) for axis in range(len(extent))]
    entries = entries.at[tuple(spot)].set(low)
    longest = extent.index(max(extent))
    spot[longest] = (spot[longest] + 1) % extent[longest]
    return entries.at[tuple(spot)].set(top_value)


def level_of(rng, dims, pieces, least, high):
    def one(position, shards_of):
        heights = jax.random.uniform(jax.random.fold_in(jax.random.fold_in(rng, 6), position), (shards_of,), jnp.float32, least / len(pieces), high / len(pieces))
        return jnp.repeat(jnp.exp(heights), dims[position] // shards_of).reshape((-1,) + (1,) * (len(dims) - position - 1))

    gain = one(*pieces[0])
    for cut in pieces[1:]:
        gain = gain * one(*cut)
    return gain


def scatter_about(rng, dims, width, limit, cuts=(), kind=jnp.bfloat16):
    values = jax.random.normal(rng, dims, jnp.float32) * width
    if len(cuts) > 0:
        values = level_of(rng, dims, cuts, -0.22, 0.18) * values
    return jnp.clip(values, min=-limit, max=limit).astype(kind)


def setup_inputs(seed: int = 0, part: int = 0) -> dict:
    splits = jax.random.split(jax.random.key(seed), 9)
    part_keys = jax.random.split(jax.random.fold_in(splits[8], part), 9)
    queries = draw_queries(jax.random.fold_in(jax.random.fold_in(splits[8], part), 71), part)
    pool = draw_pool(jax.random.fold_in(jax.random.fold_in(splits[8], part), 71), part)
    resident = scatter_about(part_keys[2], (MOVING_SEQUENCES, 2, N_CTX * RESIDENT_COUNT, KEY_VALUE_HEADS * HEAD_SIZE), 1.0, 6.0, ((2, 4), (3, 4)))
    lengths = plant(jax.random.randint(part_keys[3], (DECODE_ROWS,), PAGE_TOKENS * (RBLK - 1) + 1, PAGE_TOKENS * RBLK + 1), jax.random.fold_in(part_keys[3], 1), PAGE_TOKENS * (RBLK - 1) + 1, PAGE_TOKENS * RBLK).astype(jnp.int32)
    table = draw_table(jax.random.fold_in(jax.random.fold_in(splits[8], part), 71), part)
    moving_row_numbers = draw_moving_row_numbers(jax.random.fold_in(jax.random.fold_in(splits[8], part), 71), part)
    mover_table = draw_mover_table(jax.random.fold_in(jax.random.fold_in(splits[8], part), 71), part)
    targets = draw_targets(jax.random.fold_in(jax.random.fold_in(splits[8], part), 71), part)
    return dict(queries=queries, pool=pool, resident=resident, lengths=lengths, table=table, moving_row_numbers=moving_row_numbers, mover_table=mover_table, targets=targets)


NEG_FILL = -1e+30

def block_partial(query_per_row, key_rows, value_rows, live_mask):
    scale_factor = 1.0 / math.sqrt(HEAD_SIZE)
    scores = jnp.einsum('rkgd,rtkd->rkgt', query_per_row, key_rows.astype(jnp.float32)) * scale_factor
    live_wide = live_mask[:, None, None, :]
    scores = jnp.where(live_wide, scores, NEG_FILL)
    peak = lax.optimization_barrier(jnp.max(scores, axis=-1))
    weight = jnp.where(live_wide, jnp.exp(scores - peak[..., None]), 0.0)
    total = lax.optimization_barrier(jnp.sum(weight, axis=-1))
    rounded = lax.optimization_barrier(weight.astype(jnp.bfloat16))
    block_sum = jnp.einsum('rkgt,rtkd->rkgd', rounded.astype(jnp.float32), value_rows.astype(jnp.float32))
    return (peak, total, block_sum)

def combine(first, second):
    peak_first, total_first, acc_first = first
    peak_second, total_second, acc_second = second
    peak = jnp.maximum(peak_first, peak_second)
    scale_first = jnp.exp(peak_first - peak)
    scale_second = jnp.exp(peak_second - peak)
    total = total_first * scale_first + total_second * scale_second
    acc = acc_first * scale_first[..., None] + acc_second * scale_second[..., None]
    return (peak, total, acc)

def reference(queries, pool, resident, lengths, table, moving_row_numbers, mover_table, targets):
    query_group_size = QUERY_HEADS // KEY_VALUE_HEADS
    query_per_row = queries.astype(jnp.float32).reshape(N_CTX, SHARD_ROWS, KEY_VALUE_HEADS, query_group_size, HEAD_SIZE)
    page_entries = pool.reshape(N_CTX, POOL_PAGES, 2, PAGE_TOKENS, KEY_VALUE_HEADS, HEAD_SIZE)
    row_lengths = lengths.reshape(N_CTX, SHARD_ROWS)
    tables = table.reshape(N_CTX, SHARD_ROWS, RBLK)
    moving_query = query_per_row.reshape(DECODE_ROWS, KEY_VALUE_HEADS, query_group_size, HEAD_SIZE)[moving_row_numbers]
    held_state = resident.reshape(MOVING_SEQUENCES, 2, N_CTX, RESIDENT_COUNT, KEY_VALUE_HEADS, HEAD_SIZE)
    mover_tabs = mover_table.reshape(MOVING_SEQUENCES, N_CTX, MBLK)
    token_pos = jnp.arange(PAGE_TOKENS, dtype=jnp.int32)

    def shard_work(index):
        shard_pages = page_entries[index]
        shard_query = query_per_row[index]
        shard_lengths = row_lengths[index]
        shard_table = tables[index]
        partials = []
        for block_index in range(RBLK):
            chosen = shard_pages[shard_table[:, block_index]]
            live_mask = block_index * PAGE_TOKENS + token_pos[None, :] < shard_lengths[:, None]
            partials.append(block_partial(shard_query, chosen[:, 0], chosen[:, 1], live_mask))
        row_part = reduce(combine, partials)
        live_all = jnp.ones((MOVING_SEQUENCES, RESIDENT_COUNT), dtype=bool)
        held_parts = [block_partial(moving_query, held_state[:, 0, index], held_state[:, 1, index], live_all)]
        live_page = jnp.ones((MOVING_SEQUENCES, PAGE_TOKENS), dtype=bool)
        shard_movers = lax.dynamic_index_in_dim(mover_tabs, index, 1, keepdims=False)
        for block_index in range(MBLK):
            chosen = shard_pages[shard_movers[:, block_index]]
            held_parts.append(block_partial(moving_query, chosen[:, 0], chosen[:, 1], live_page))
        return (row_part, reduce(combine, held_parts))
    row_parts, held_parts = lax.map(shard_work, jnp.arange(N_CTX, dtype=jnp.int32))
    held_peaks, held_totals, held_sums = held_parts
    held_top = lax.optimization_barrier(jnp.max(held_peaks, axis=0))
    held_scale = jnp.exp(held_peaks - held_top[None])
    held_total = lax.optimization_barrier(jnp.sum(held_totals * held_scale, axis=0))
    held_sum = lax.optimization_barrier(jnp.sum(held_sums * held_scale[..., None], axis=0))
    row_peak, row_total, row_acc = [part.reshape((DECODE_ROWS,) + part.shape[2:]) for part in row_parts]
    extra_peak = jnp.full(row_peak.shape, NEG_FILL, jnp.float32).at[moving_row_numbers].set(held_top)
    extra_total = jnp.zeros(row_total.shape, jnp.float32).at[moving_row_numbers].set(held_total)
    extra_acc = jnp.zeros(row_acc.shape, jnp.float32).at[moving_row_numbers].set(held_sum)
    peak, total, acc = combine((row_peak, row_total, row_acc), (extra_peak, extra_total, extra_acc))
    attended = (acc / total[..., None]).reshape(DECODE_ROWS, QUERY_HEADS * HEAD_SIZE).astype(jnp.bfloat16)
    count = MOVING_SEQUENCES * MBLK
    shard_ids = jnp.arange(N_CTX, dtype=jnp.int32)
    shard_targets = targets.reshape(MOVING_SEQUENCES, N_CTX, MBLK).transpose(1, 0, 2).reshape(N_CTX, count)
    offsets = jnp.mod(shard_targets - shard_ids[:, None], N_CTX)
    order = jnp.arange(count, dtype=jnp.int32)
    earlier = order[None, :] < order[:, None]
    same = offsets[:, :, None] == offsets[:, None, :]
    rank = lax.optimization_barrier(jnp.sum((same & earlier[None]).astype(jnp.int32), axis=2))
    home = jnp.mod(shard_ids[:, None] + offsets, N_CTX)
    slot = home * ARRIVAL_SLOTS + offsets * CAP + rank
    mover_pages = mover_tabs.transpose(1, 0, 2).reshape(N_CTX, count)
    anchor = shard_ids[:, None] * POOL_PAGES + mover_pages
    received = jnp.zeros((N_CTX * ARRIVAL_SLOTS, 2, PAGE_TOKENS, KEY_VALUE_HEADS * HEAD_SIZE), jnp.bfloat16)
    received = received.at[slot.reshape(-1)].set(pool[anchor.reshape(-1)])
    return (attended, received)
```

```python
import functools
import math

import jax
import jax.numpy as jnp
from jax import lax
from jax.experimental import pallas as pl
from jax.experimental.pallas import tpu as pltpu
from jax.sharding import PartitionSpec as P

QUERY_HEADS = 40
KEY_VALUE_HEADS = 8
HEAD_SIZE = 128
PAGE_TOKENS = 128
REACH = 3
CAP = 2
ARRIVAL_SLOTS = 6
HEAD_ROWS = 16
POOL_PIECES = 4

NEG_FILL = -1e30
MESH = pl.DeviceIdType.MESH


def block_partial(query, keys, values, live):
    scores = lax.dot_general(
        query, keys, (((1,), (1,)), ((), ())), preferred_element_type=jnp.float32
    ) * (1.0 / math.sqrt(HEAD_SIZE))
    if live is not None:
        scores = jnp.where(live, scores, NEG_FILL)
    peak = jnp.max(scores, axis=1, keepdims=True)
    weight = jnp.exp(scores - peak)
    if live is not None:
        weight = jnp.where(live, weight, 0.0)
    total = jnp.sum(weight, axis=1, keepdims=True)
    acc = jnp.dot(weight.astype(jnp.bfloat16), values, preferred_element_type=jnp.float32)
    return peak, total, acc


def combine(first, second):
    peak = jnp.maximum(first[0], second[0])
    scale_first = jnp.exp(first[0] - peak)
    scale_second = jnp.exp(second[0] - peak)
    return (
        peak,
        first[1] * scale_first + second[1] * scale_second,
        first[2] * scale_first + second[2] * scale_second,
    )


def kernel(
    n, group,
    lengths, table, moving, mover_table, targets, q_ref, pool_hbm, resident_hbm,
    attended, received,
    pool, resident, stage, heads, asked, parts, result,
    pool_sem, resident_sem, keep_sem, page_send, page_recv, ask_send, ask_recv, part_send, part_recv,
):
    rows = q_ref.shape[0]
    head_count = q_ref.shape[1] // HEAD_SIZE
    pages = pool_hbm.shape[0]
    movers = moving.shape[0]
    me = lax.axis_index("ctx")

    def peer_at(step):
        return lax.rem(me + step, n)

    def each_peer(act):
        if n <= 8:
            for step in range(1, n):
                act(step)
        else:
            pl.loop(1, n)(act)

    piece = pages // POOL_PIECES
    fetches = [
        pltpu.make_async_copy(
            pool_hbm.at[pl.ds(i * piece, piece)], pool.at[pl.ds(i * piece, piece)], pool_sem.at[i]
        )
        for i in range(POOL_PIECES)
    ]
    fetch_resident = pltpu.make_async_copy(resident_hbm, resident, resident_sem)
    for fetch in fetches:
        fetch.start()
    fetch_resident.start()

    barrier = pltpu.get_barrier_semaphore()

    def greet(step):
        pl.semaphore_signal(barrier, inc=1, device_id={"ctx": peer_at(step)}, device_id_type=MESH)

    each_peer(greet)

    heads[...] = jnp.zeros_like(heads)
    for h in range(head_count):
        heads[:, h, :] = q_ref[:, h * HEAD_SIZE : (h + 1) * HEAD_SIZE].astype(jnp.float32)
    pool[pages] = jnp.zeros(pool.shape[1:], pool.dtype)
    for g in range(movers):
        place = jnp.clip(moving[g] - me * rows, 0, rows - 1)
        asked[me, g] = heads[place].astype(jnp.bfloat16)

    pl.semaphore_wait(barrier, n - 1)

    def ask(step):
        return pltpu.make_async_remote_copy(
            src_ref=asked.at[me], dst_ref=asked.at[me],
            send_sem=ask_send.at[step], recv_sem=ask_recv.at[step],
            device_id={"ctx": peer_at(step)}, device_id_type=MESH,
        )

    each_peer(lambda step: ask(step).start())

    named = [(g, b) for g in range(movers) for b in range(mover_table.shape[1])]
    offsets = [lax.rem(targets[g, b] - me + n, n) for g, b in named]
    slots = []
    for i, offset in enumerate(offsets):
        rank = jnp.int32(0)
        for before in offsets[:i]:
            rank = rank + jnp.where(before == offset, 1, 0)
        slots.append(offset * CAP + rank)

    def page_of(slot):
        page = jnp.int32(pages)
        for (g, b), taken in zip(named, slots):
            page = jnp.where(taken == slot, mover_table[g, b], page)
        return page

    def page_copy(offset, rank):
        slot = offset * CAP + rank
        return pltpu.make_async_remote_copy(
            src_ref=stage.at[slot], dst_ref=received.at[slot],
            send_sem=page_send.at[slot], recv_sem=page_recv.at[slot],
            device_id={"ctx": peer_at(offset)}, device_id_type=MESH,
        )

    for fetch in fetches:
        fetch.wait()
    page_copies = []
    for offset in range(REACH - 1, 0, -1):
        for rank in range(CAP):
            slot = offset * CAP + rank
            stage[slot] = pool[page_of(slot)]
            copy = page_copy(offset, rank)
            copy.start()
            page_copies.append(copy)
    for slot in range(CAP):
        stage[slot] = pool[page_of(slot)]
    keep = pltpu.make_async_copy(
        stage.at[pl.ds(0, CAP)], received.at[pl.ds(0, CAP)], keep_sem
    )
    keep.start()

    head = lax.broadcasted_iota(jnp.int32, (HEAD_ROWS, HEAD_SIZE), 0)
    token = lax.broadcasted_iota(jnp.int32, (HEAD_ROWS, PAGE_TOKENS), 1)
    upper = head < group

    def spread(query):
        query = query.astype(jnp.float32)
        return jnp.concatenate(
            [jnp.where(upper, query, 0.0), jnp.where(upper, 0.0, query)], axis=1
        ).astype(jnp.bfloat16)

    def own_half(state):
        peak, total, acc = state
        return peak, total, jnp.where(upper, acc[:, :HEAD_SIZE], acc[:, HEAD_SIZE:])

    states = []
    for row in range(rows):
        query = spread(heads[row])
        blocks = []
        for b in range(table.shape[1]):
            page = table[row, b]
            live = b * PAGE_TOKENS + token < lengths[row]
            blocks.append(block_partial(query, pool[page, 0], pool[page, 1], live))
        states.append(own_half(functools.reduce(combine, blocks)))

    fetch_resident.wait()
    each_peer(lambda step: ask(step).wait_recv())
    lane = lax.broadcasted_iota(jnp.int32, (HEAD_ROWS, HEAD_SIZE), 1)
    for g in range(movers):
        owner = lax.div(moving[g], jnp.int32(rows))
        query = spread(asked[owner, g])
        blocks = [block_partial(query, resident[g, 0], resident[g, 1], None)]
        for b in range(mover_table.shape[1]):
            page = mover_table[g, b]
            blocks.append(block_partial(query, pool[page, 0], pool[page, 1], None))
        peak, total, acc = own_half(functools.reduce(combine, blocks))
        parts[me, g, 0] = acc
        parts[me, g, 1] = jnp.where(lane < HEAD_SIZE // 2, peak, total)

    def tell(step):
        return pltpu.make_async_remote_copy(
            src_ref=parts.at[me], dst_ref=parts.at[me],
            send_sem=part_send.at[step], recv_sem=part_recv.at[step],
            device_id={"ctx": peer_at(step)}, device_id_type=MESH,
        )

    each_peer(lambda step: tell(step).start())
    each_peer(lambda step: tell(step).wait_recv())

    def part_of(source, g):
        stats = parts[source, g, 1]
        return stats[:, :1], stats[:, HEAD_SIZE // 2 : HEAD_SIZE // 2 + 1], parts[source, g, 0]

    merged = []
    for g in range(movers):
        if n <= 8:
            merged.append(functools.reduce(combine, [part_of(e, g) for e in range(n)]))
        else:
            merged.append(
                lax.fori_loop(
                    1, n, lambda e, state, g=g: combine(state, part_of(e, g)), part_of(0, g)
                )
            )
    for row in range(rows):
        peak, total, acc = (
            jnp.full((HEAD_ROWS, 1), NEG_FILL, jnp.float32),
            jnp.zeros((HEAD_ROWS, 1), jnp.float32),
            jnp.zeros((HEAD_ROWS, HEAD_SIZE), jnp.float32),
        )
        for g in range(movers):
            here = moving[g] - me * rows - row
            narrow = jnp.broadcast_to(here, (HEAD_ROWS, 1)) == 0
            wide = jnp.broadcast_to(here, (HEAD_ROWS, HEAD_SIZE)) == 0
            peak = jnp.where(narrow, merged[g][0], peak)
            total = jnp.where(narrow, merged[g][1], total)
            acc = jnp.where(wide, merged[g][2], acc)
        peak, total, acc = combine(states[row], (peak, total, acc))
        result[row] = acc / total
    for h in range(head_count):
        attended[:, h * HEAD_SIZE : (h + 1) * HEAD_SIZE] = result[:, h, :].astype(attended.dtype)

    each_peer(lambda step: ask(step).wait_send())
    each_peer(lambda step: tell(step).wait_send())
    keep.wait()
    for copy in page_copies:
        copy.wait()


def body(queries, pool, resident, lengths, table, moving_row_numbers, mover_table, targets):
    n = lax.axis_size("ctx")
    rows, width = queries.shape
    pages = pool.shape[0]
    movers = moving_row_numbers.shape[0]
    smem = pl.BlockSpec(memory_space=pltpu.SMEM)
    vmem = pl.BlockSpec(memory_space=pltpu.VMEM)
    anywhere = pl.BlockSpec(memory_space=pl.ANY)
    page_shape = pool.shape[1:]
    return pl.pallas_call(
        functools.partial(kernel, n, QUERY_HEADS // KEY_VALUE_HEADS),
        out_shape=(
            jax.ShapeDtypeStruct((rows, width), jnp.bfloat16),
            jax.ShapeDtypeStruct((ARRIVAL_SLOTS,) + page_shape, jnp.bfloat16),
        ),
        in_specs=[smem] * 5 + [vmem, anywhere, anywhere],
        out_specs=(vmem, anywhere),
        scratch_shapes=[
            pltpu.VMEM((pages + 1,) + page_shape, jnp.bfloat16),
            pltpu.VMEM(resident.shape, jnp.bfloat16),
            pltpu.VMEM((ARRIVAL_SLOTS,) + page_shape, jnp.bfloat16),
            pltpu.VMEM((rows, HEAD_ROWS, HEAD_SIZE), jnp.float32),
            pltpu.VMEM((n, movers, HEAD_ROWS, HEAD_SIZE), jnp.bfloat16),
            pltpu.VMEM((n, movers, 2, HEAD_ROWS, HEAD_SIZE), jnp.float32),
            pltpu.VMEM((rows, HEAD_ROWS, HEAD_SIZE), jnp.float32),
            pltpu.SemaphoreType.DMA((POOL_PIECES,)),
            pltpu.SemaphoreType.DMA,
            pltpu.SemaphoreType.DMA,
            pltpu.SemaphoreType.DMA((ARRIVAL_SLOTS,)),
            pltpu.SemaphoreType.DMA((ARRIVAL_SLOTS,)),
            pltpu.SemaphoreType.DMA((n,)),
            pltpu.SemaphoreType.DMA((n,)),
            pltpu.SemaphoreType.DMA((n,)),
            pltpu.SemaphoreType.DMA((n,)),
        ],
        compiler_params=pltpu.CompilerParams(
            collective_id=0, has_side_effects=True, vmem_limit_bytes=32 * 1024 * 1024
        ),
    )(lengths, table, moving_row_numbers, mover_table, targets, queries, pool, resident)


def solution(mesh):
    in_specs = (
        P(("groups", "ctx"), "tp"),
        P(("groups", "ctx"), None, None, "tp"),
        P("groups", None, "ctx", "tp"),
        P(("groups", "ctx")),
        P(("groups", "ctx"), None),
        P("groups"),
        P("groups", "ctx"),
        P("groups", "ctx"),
    )
    out_specs = (P(("groups", "ctx"), "tp"), P(("groups", "ctx"), None, None, "tp"))
    return jax.shard_map(body, mesh=mesh, in_specs=in_specs, out_specs=out_specs, check_vma=False)
```

```python
import functools
import math

import jax
import jax.numpy as jnp
from jax import lax
from jax.experimental import pallas as pl
from jax.experimental.pallas import tpu as pltpu
from jax.sharding import PartitionSpec as P

QUERY_HEADS = 40
KEY_VALUE_HEADS = 8
HEAD_SIZE = 128
PAGE_TOKENS = 128
REACH = 3
CAP = 2
ARRIVAL_SLOTS = 6
HEAD_ROWS = 16
POOL_PIECES = 4
VMEM_BYTES = 60 * 1024 * 1024

NEG_FILL = -1e30
MESH = pl.DeviceIdType.MESH


def block_partials(queries, keys, values, live, own_half):
    scores = [
        lax.dot_general(q, k, (((1,), (1,)), ((), ())), preferred_element_type=jnp.float32)
        for q, k in zip(queries, keys)
    ]
    scores = jnp.concatenate(scores, axis=0) * (1.0 / math.sqrt(HEAD_SIZE))
    if live is not None:
        scores = jnp.where(live, scores, NEG_FILL)
    peak = jnp.max(scores, axis=1, keepdims=True)
    weight = jnp.exp(scores - peak)
    if live is not None:
        weight = jnp.where(live, weight, 0.0)
    total = jnp.sum(weight, axis=1, keepdims=True)
    weight = weight.astype(jnp.bfloat16)
    sums = [
        own_half(
            jnp.dot(
                weight[i * HEAD_ROWS : (i + 1) * HEAD_ROWS], v, preferred_element_type=jnp.float32
            )
        )
        for i, v in enumerate(values)
    ]
    return peak, total, jnp.concatenate(sums, axis=0)


def joined(state, count):
    size = state[0].shape[0] // count
    return functools.reduce(
        combine, [tuple(a[i * size : (i + 1) * size] for a in state) for i in range(count)]
    )


def combine(first, second):
    peak = jnp.maximum(first[0], second[0])
    scale_first = jnp.exp(first[0] - peak)
    scale_second = jnp.exp(second[0] - peak)
    return (
        peak,
        first[1] * scale_first + second[1] * scale_second,
        first[2] * scale_first + second[2] * scale_second,
    )


def kernel(
    n, group,
    lengths, table, moving, mover_table, targets, q_ref, pool_hbm, resident_hbm,
    attended, received,
    pool, resident, stage, heads, asked, parts, result,
    pool_sem, resident_sem, keep_sem, page_send, page_recv, ask_send, ask_recv, part_send, part_recv,
):
    rows = q_ref.shape[0]
    head_count = q_ref.shape[1] // HEAD_SIZE
    pages = pool_hbm.shape[0]
    movers = moving.shape[0]
    me = lax.axis_index("ctx")

    def peer_at(step):
        return lax.rem(me + step, n)

    def each_peer(act):
        if n <= 8:
            for step in range(1, n):
                act(step)
        else:
            pl.loop(1, n)(act)

    piece = pages // POOL_PIECES
    fetches = [
        pltpu.make_async_copy(
            pool_hbm.at[pl.ds(i * piece, piece)], pool.at[pl.ds(i * piece, piece)], pool_sem.at[i]
        )
        for i in range(POOL_PIECES)
    ]
    fetch_resident = pltpu.make_async_copy(resident_hbm, resident, resident_sem)
    for fetch in fetches:
        fetch.start()
    fetch_resident.start()

    barrier = pltpu.get_barrier_semaphore()

    def greet(step):
        pl.semaphore_signal(barrier, inc=1, device_id={"ctx": peer_at(step)}, device_id_type=MESH)

    each_peer(greet)

    heads[...] = jnp.zeros_like(heads)
    for h in range(head_count):
        heads[:, h, :] = q_ref[:, h * HEAD_SIZE : (h + 1) * HEAD_SIZE].astype(jnp.float32)
    pool[pages] = jnp.zeros(pool.shape[1:], pool.dtype)
    for g in range(movers):
        place = jnp.clip(moving[g] - me * rows, 0, rows - 1)
        asked[me, g] = heads[place].astype(jnp.bfloat16)

    pl.semaphore_wait(barrier, n - 1)

    def ask(step):
        return pltpu.make_async_remote_copy(
            src_ref=asked.at[me], dst_ref=asked.at[me],
            send_sem=ask_send.at[step], recv_sem=ask_recv.at[step],
            device_id={"ctx": peer_at(step)}, device_id_type=MESH,
        )

    each_peer(lambda step: ask(step).start())

    named = [(g, b) for g in range(movers) for b in range(mover_table.shape[1])]
    offsets = [lax.rem(targets[g, b] - me + n, n) for g, b in named]
    slots = []
    for i, offset in enumerate(offsets):
        rank = jnp.int32(0)
        for before in offsets[:i]:
            rank = rank + jnp.where(before == offset, 1, 0)
        slots.append(offset * CAP + rank)

    def page_of(slot):
        page = jnp.int32(pages)
        for (g, b), taken in zip(named, slots):
            page = jnp.where(taken == slot, mover_table[g, b], page)
        return page

    def page_copy(offset, rank):
        slot = offset * CAP + rank
        return pltpu.make_async_remote_copy(
            src_ref=stage.at[slot], dst_ref=received.at[slot],
            send_sem=page_send.at[slot], recv_sem=page_recv.at[slot],
            device_id={"ctx": peer_at(offset)}, device_id_type=MESH,
        )

    for fetch in fetches:
        fetch.wait()
    page_copies = []
    for offset in range(REACH - 1, 0, -1):
        for rank in range(CAP):
            slot = offset * CAP + rank
            stage[slot] = pool[page_of(slot)]
            copy = page_copy(offset, rank)
            copy.start()
            page_copies.append(copy)
    for slot in range(CAP):
        stage[slot] = pool[page_of(slot)]
    keep = pltpu.make_async_copy(
        stage.at[pl.ds(0, CAP)], received.at[pl.ds(0, CAP)], keep_sem
    )
    keep.start()

    head = lax.broadcasted_iota(jnp.int32, (HEAD_ROWS, HEAD_SIZE), 0)
    token = lax.broadcasted_iota(jnp.int32, (HEAD_ROWS, PAGE_TOKENS), 1)
    upper = head < group

    def spread(query):
        query = query.astype(jnp.float32)
        return jnp.concatenate(
            [jnp.where(upper, query, 0.0), jnp.where(upper, 0.0, query)], axis=1
        ).astype(jnp.bfloat16)

    def own_half(acc):
        return jnp.where(upper, acc[:, :HEAD_SIZE], acc[:, HEAD_SIZE:])

    fetch_resident.wait()
    each_peer(lambda step: ask(step).wait_recv())
    lane = lax.broadcasted_iota(jnp.int32, (HEAD_ROWS, HEAD_SIZE), 1)
    owners = [lax.div(moving[g], jnp.int32(rows)) for g in range(movers)]
    queries = [spread(asked[owners[g], g]) for g in range(movers)]
    held = mover_table.shape[1] + 1
    keys = [resident[g, 0] for g in range(movers)]
    values = [resident[g, 1] for g in range(movers)]
    for b in range(held - 1):
        for g in range(movers):
            keys.append(pool[mover_table[g, b], 0])
            values.append(pool[mover_table[g, b], 1])
    state = joined(block_partials(queries * held, keys, values, None, own_half), held)
    for g in range(movers):
        peak, total, acc = (a[g * HEAD_ROWS : (g + 1) * HEAD_ROWS] for a in state)
        parts[me, g * head_count : (g + 1) * head_count] = acc[:head_count]
        for i, column in enumerate((peak, total)):
            at = movers * head_count + 2 * g + i
            parts[me, at : at + 1] = jnp.sum(jnp.where(lane == head, column, 0.0), axis=0, keepdims=True)

    def tell(step):
        return pltpu.make_async_remote_copy(
            src_ref=parts.at[me], dst_ref=parts.at[me],
            send_sem=part_send.at[step], recv_sem=part_recv.at[step],
            device_id={"ctx": peer_at(step)}, device_id_type=MESH,
        )

    each_peer(lambda step: tell(step).start())

    queries = [spread(heads[row]) for row in range(rows)]
    own_blocks = table.shape[0]
    places = [(b, row) for b in range(own_blocks) for row in range(rows)]
    keys = [pool[table[b, row], 0] for b, row in places]
    values = [pool[table[b, row], 1] for b, row in places]
    live = jnp.concatenate(
        [b * PAGE_TOKENS + token < lengths[row] for b, row in places], axis=0
    )
    state = joined(block_partials(queries * own_blocks, keys, values, live, own_half), own_blocks)

    each_peer(lambda step: tell(step).wait_recv())

    def part_of(source, g):
        at = movers * head_count + 2 * g
        peak, total = (
            jnp.sum(jnp.where(lane == head, parts[source, i : i + 1], 0.0), axis=1, keepdims=True)
            for i in (at, at + 1)
        )
        acc = parts[source, g * head_count : (g + 1) * head_count]
        padding = jnp.zeros((HEAD_ROWS - head_count, HEAD_SIZE), jnp.float32)
        return peak, total, jnp.concatenate([acc, padding], axis=0)

    merged = []
    for g in range(movers):
        if n <= 8:
            merged.append(functools.reduce(combine, [part_of(e, g) for e in range(n)]))
        else:
            merged.append(
                lax.fori_loop(
                    1, n, lambda e, state, g=g: combine(state, part_of(e, g)), part_of(0, g)
                )
            )
    def row_of(width):
        return lax.div(lax.broadcasted_iota(jnp.int32, (rows * HEAD_ROWS, width), 0), HEAD_ROWS)

    def down(part):
        return jnp.concatenate([part] * rows, axis=0)

    extra = (
        jnp.full((rows * HEAD_ROWS, 1), NEG_FILL, jnp.float32),
        jnp.zeros((rows * HEAD_ROWS, 1), jnp.float32),
        jnp.zeros((rows * HEAD_ROWS, HEAD_SIZE), jnp.float32),
    )
    for g in range(movers):
        place = moving[g] - me * rows
        extra = tuple(
            jnp.where(row_of(old.shape[1]) == place, down(new), old)
            for new, old in zip(merged[g], extra)
        )
    peak, total, acc = combine(state, extra)
    result[...] = (acc / total).reshape(result.shape)
    for h in range(head_count):
        attended[:, h * HEAD_SIZE : (h + 1) * HEAD_SIZE] = result[:, h, :].astype(attended.dtype)

    each_peer(lambda step: ask(step).wait_send())
    each_peer(lambda step: tell(step).wait_send())
    keep.wait()
    for copy in page_copies:
        copy.wait()


def body(queries, pool, resident, lengths, table, moving_row_numbers, mover_table, targets):
    n = lax.axis_size("ctx")
    rows, width = queries.shape
    pages = pool.shape[0]
    movers = moving_row_numbers.shape[0]
    smem = pl.BlockSpec(memory_space=pltpu.SMEM)
    vmem = pl.BlockSpec(memory_space=pltpu.VMEM)
    anywhere = pl.BlockSpec(memory_space=pl.ANY)
    page_shape = pool.shape[1:]
    part_rows = -(-movers * (width // HEAD_SIZE + 2) // 8) * 8
    return pl.pallas_call(
        functools.partial(kernel, n, QUERY_HEADS // KEY_VALUE_HEADS),
        out_shape=(
            jax.ShapeDtypeStruct((rows, width), jnp.bfloat16),
            jax.ShapeDtypeStruct((ARRIVAL_SLOTS,) + page_shape, jnp.bfloat16),
        ),
        in_specs=[smem] * 5 + [vmem, anywhere, anywhere],
        out_specs=(vmem, anywhere),
        scratch_shapes=[
            pltpu.VMEM((pages + 1,) + page_shape, jnp.bfloat16),
            pltpu.VMEM(resident.shape, jnp.bfloat16),
            pltpu.VMEM((ARRIVAL_SLOTS,) + page_shape, jnp.bfloat16),
            pltpu.VMEM((rows, HEAD_ROWS, HEAD_SIZE), jnp.float32),
            pltpu.VMEM((n, movers, HEAD_ROWS, HEAD_SIZE), jnp.bfloat16),
            pltpu.VMEM((n, part_rows, HEAD_SIZE), jnp.float32),
            pltpu.VMEM((rows, HEAD_ROWS, HEAD_SIZE), jnp.float32),
            pltpu.SemaphoreType.DMA((POOL_PIECES,)),
            pltpu.SemaphoreType.DMA,
            pltpu.SemaphoreType.DMA,
            pltpu.SemaphoreType.DMA((ARRIVAL_SLOTS,)),
            pltpu.SemaphoreType.DMA((ARRIVAL_SLOTS,)),
            pltpu.SemaphoreType.DMA((n,)),
            pltpu.SemaphoreType.DMA((n,)),
            pltpu.SemaphoreType.DMA((n,)),
            pltpu.SemaphoreType.DMA((n,)),
        ],
        compiler_params=pltpu.CompilerParams(
            collective_id=0, has_side_effects=True, vmem_limit_bytes=VMEM_BYTES
        ),
    )(lengths, table.T, moving_row_numbers, mover_table, targets, queries, pool, resident)


def solution(mesh):
    in_specs = (
        P(("groups", "ctx"), "tp"),
        P(("groups", "ctx"), None, None, "tp"),
        P("groups", None, "ctx", "tp"),
        P(("groups", "ctx")),
        P(("groups", "ctx"), None),
        P("groups"),
        P("groups", "ctx"),
        P("groups", "ctx"),
    )
    out_specs = (P(("groups", "ctx"), "tp"), P(("groups", "ctx"), None, None, "tp"))
    return jax.shard_map(body, mesh=mesh, in_specs=in_specs, out_specs=out_specs, check_vma=False)
```
